32 devices in a mesh: replica: 4 (over z), shard: 4 (over y, core), ctx: 2 (over x).
Axes of the slice: x: 2, y: 2, z: 4, core: 2. Of those that a mesh axis runs over, the one named last changes fastest.
Arguments:
- tokens: bfloat16 [16, 1024, 768], P(('replica', 'shard'), 'ctx'), may hold values from -6 to 6
- norm_gain_one: bfloat16 [2, 768], P(None, ('shard', 'ctx')), may hold values from 0.5 to 1.5
- norm_shift_one: bfloat16 [2, 768], P(None, ('shard', 'ctx')), may hold values from -1.25 to 1.25
- norm_gain_two: bfloat16 [2, 768], P(None, ('shard', 'ctx')), may hold values from 0.5 to 1.5
- norm_shift_two: bfloat16 [2, 768], P(None, ('shard', 'ctx')), may hold values from -1.25 to 1.25
- attn_in_weight: bfloat16 [2, 768, 2304], P(None, ('shard', 'ctx')), may hold values from -0.3125 to 0.3125
- attn_in_bias: bfloat16 [2, 2304], P(None, ('shard', 'ctx')), may hold values from -1.75 to 1.75
- attn_out_weight: bfloat16 [2, 768, 768], P(None, ('shard', 'ctx')), may hold values from -1.25 to 1.25
- attn_out_bias: bfloat16 [2, 768], P(None, ('shard', 'ctx')), may hold values from -1.25 to 1.25
- mlp_in_weight: bfloat16 [2, 768, 3072], P(None, ('shard', 'ctx')), may hold values from -0.21875 to 0.21875
- mlp_in_bias: bfloat16 [2, 3072], P(None, ('shard', 'ctx')), may hold values from -1.75 to 1.75
- mlp_out_weight: bfloat16 [2, 3072, 768], P(None, ('shard', 'ctx')), may hold values from -0.109375 to 0.109375
- mlp_out_bias: bfloat16 [2, 768], P(None, ('shard', 'ctx')), may hold values from -1.25 to 1.25
- cotangent: bfloat16 [16, 1024, 768], P(('replica', 'shard'), 'ctx'), may hold values from -6 to 6
Outputs:
- output: bfloat16 [16, 1024, 768], P(('replica', 'shard'), 'ctx')
- input_grad: bfloat16 [16, 1024, 768], P(('replica', 'shard'), 'ctx')
- grad_norm_gain_one: float32 [2, 768], P(None, ('shard', 'ctx'))
- grad_norm_shift_one: float32 [2, 768], P(None, ('shard', 'ctx'))
- grad_norm_gain_two: float32 [2, 768], P(None, ('shard', 'ctx'))
- grad_norm_shift_two: float32 [2, 768], P(None, ('shard', 'ctx'))
- grad_attn_in_weight: float32 [2, 768, 2304], P(None, ('shard', 'ctx'))
- grad_attn_in_bias: float32 [2, 2304], P(None, ('shard', 'ctx'))
- grad_attn_out_weight: float32 [2, 768, 768], P(None, ('shard', 'ctx'))
- grad_attn_out_bias: float32 [2, 768], P(None, ('shard', 'ctx'))
- grad_mlp_in_weight: float32 [2, 768, 3072], P(None, ('shard', 'ctx'))
- grad_mlp_in_bias: float32 [2, 3072], P(None, ('shard', 'ctx'))
- grad_mlp_out_weight: float32 [2, 3072, 768], P(None, ('shard', 'ctx'))
- grad_mlp_out_bias: float32 [2, 768], P(None, ('shard', 'ctx'))
The draws below stay inside these ranges and needn't reach their ends.
All inputs are finite; a program needn't handle non-finite values.
Results may differ from the reference program's by a relative error of at most 0.03.
The reference program's roundings to bfloat16 on the way count: a program that leaves them out, or rounds other values in their place, can miss the bound.
Values may be sent and summed in bfloat16 or wider, within the bound.
A program may use at most 320 MiB of HBM per device.

```python
import jax
import jax.numpy as jnp
from jax import lax

D = 768
HEADS = 12
HEAD_DIM = 64
ROT = 16
FF = 3072
LAYERS = 2
SEQS = 1
LEN = 1024
SEQUENCES = 16


def block_levels(stream_key, extent, split, low, largest):
    loudness, own = 1.0, jax.random.fold_in(stream_key, 6)
    for axis_at, parts in split:
        heights = jnp.exp(jax.random.uniform(jax.random.fold_in(own, axis_at), (parts,), jnp.float32, low / len(split), largest / len(split)))
        loudness = loudness * jnp.repeat(heights, extent[axis_at] // parts).reshape([-1 if axis == axis_at else 1 for axis in range(len(extent))])
    return loudness


def bell_draw(rng, shape, width, limit, pieces=(), kind=jnp.bfloat16):
    drawn = width * jax.random.normal(rng, shape, jnp.float32)
    if pieces:
        drawn = drawn * block_levels(rng, shape, pieces, -0.22, 0.18)
    return jnp.clip(drawn, -limit, limit).astype(kind)


def setup_inputs(seed: int = 0) -> dict:
    streams_of = jax.random.split(jax.random.key(seed), 15)
    return {
        "tokens": bell_draw(streams_of[0], (SEQUENCES, LEN, D), 1.0, 6.0, ((0, 16), (1, 2))),
        "norm_gain_one": jnp.clip(1.0 + 0.1 * jax.random.normal(streams_of[1], (LAYERS, D), jnp.float32), 0.5, 1.5).astype(jnp.bfloat16),
        "norm_shift_one": bell_draw(streams_of[2], (LAYERS, D), 0.2, 1.25, ((1, 8),)),
        "norm_gain_two": jnp.clip(1.0 + 0.1 * jax.random.normal(streams_of[3], (LAYERS, D), jnp.float32), 0.5, 1.5).astype(jnp.bfloat16),
        "norm_shift_two": bell_draw(streams_of[4], (LAYERS, D), 0.2, 1.25, ((1, 8),)),
        "attn_in_weight": bell_draw(streams_of[5], (LAYERS, D, 3 * D), (D // 2) ** -0.5, 0.3125, ((1, 8),)),
        "attn_in_bias": bell_draw(streams_of[6], (LAYERS, 3 * D), 0.3, 1.75, ((1, 8),)),
        "attn_out_weight": bell_draw(streams_of[7], (LAYERS, D, D), (D // 32) ** -0.5, 1.25, ((1, 8),)),
        "attn_out_bias": bell_draw(streams_of[8], (LAYERS, D), 0.2, 1.25, ((1, 8),)),
        "mlp_in_weight": bell_draw(streams_of[9], (LAYERS, D, FF), D ** -0.5, 0.21875, ((1, 8),)),
        "mlp_in_bias": bell_draw(streams_of[10], (LAYERS, FF), 0.3, 1.75, ((1, 8),)),
        "mlp_out_weight": bell_draw(streams_of[11], (LAYERS, FF, D), FF ** -0.5, 0.109375, ((1, 8),)),
        "mlp_out_bias": bell_draw(streams_of[12], (LAYERS, D), 0.2, 1.25, ((1, 8),)),
        "cotangent": bell_draw(streams_of[13], (SEQUENCES, LEN, D), 1.0, 6.0, ((0, 16), (1, 2))),
    }


@jax.custom_vjp
def low(v):
    return lax.optimization_barrier(v.astype(jnp.bfloat16)).astype(jnp.float32)

@jax.custom_vjp
def low_back(v):
    return v

def low_keep(v):
    return (low(v), None)

def low_pass(kept, grad):
    return (grad,)

def back_keep(v):
    return (v, None)

def back_low(kept, grad):
    return (low(grad),)
low.defvjp(low_keep, low_pass)
low_back.defvjp(back_keep, back_low)
highest = lax.Precision.HIGHEST
epsilon = 1e-05

def layer_norm(values, gain, shift):
    centre = lax.optimization_barrier(jnp.mean(values, axis=-1, keepdims=True))
    centred = values - centre
    spread = lax.optimization_barrier(jnp.mean(centred * centred, axis=-1, keepdims=True))
    return centred * lax.rsqrt(spread + epsilon) * gain + shift

def rotary(values, positions):
    half_rot = ROT // 2
    inverse = 1.0 / 10000.0 ** (jnp.arange(half_rot, dtype=jnp.float32) * 2.0 / ROT)
    angles = positions.astype(jnp.float32)[:, None] * inverse[None, :]
    angles = jnp.concatenate([angles, angles], axis=-1)[:, None, :]
    cosine = jnp.cos(angles)
    sine = jnp.sin(angles)
    rot_part = values[..., :ROT]
    first_half = rot_part[..., :half_rot]
    second_half = rot_part[..., half_rot:]
    turned = jnp.concatenate([-second_half, first_half], axis=-1)
    return jnp.concatenate([rot_part * cosine + turned * sine, values[..., ROT:]], axis=-1)

def matmul(left, right):
    return jnp.matmul(left, right, precision=highest)

def layer(hidden, params):
    gain_one, shift_one, gain_two, shift_two, in_weight, in_bias, out_weight, out_bias, up_weight, up_bias, down_weight, down_bias = params
    batch_count = hidden.shape[0]
    seq_length = hidden.shape[1]
    normed_one = low(layer_norm(hidden, gain_one, shift_one))
    projected = low_back(matmul(normed_one, in_weight) + in_bias)
    split_heads = projected.reshape(batch_count, seq_length, 3, HEADS, HEAD_DIM)
    positions = jnp.arange(seq_length, dtype=jnp.int32)
    query_heads = low(rotary(split_heads[:, :, 0], positions))
    key_heads = low(rotary(split_heads[:, :, 1], positions))
    value_heads = low(split_heads[:, :, 2])
    scores = low_back(jnp.einsum('bqhd,bkhd->bhqk', query_heads, key_heads, precision=highest)) * HEAD_DIM ** (-0.5)
    causal = positions[:, None] >= positions[None, :]
    scores = jnp.where(causal, scores, -jnp.inf)
    chances = low(jax.nn.softmax(scores, axis=-1))
    context = jnp.einsum('bhqk,bkhd->bqhd', chances, value_heads, precision=highest)
    context = low(low_back(context)).reshape(batch_count, seq_length, HEADS * HEAD_DIM)
    attn_branch = matmul(context, out_weight) + out_bias
    normed_two = low(layer_norm(hidden, gain_two, shift_two))
    pre_active = low_back(matmul(normed_two, up_weight) + up_bias)
    active = low(jax.nn.gelu(pre_active, approximate=False))
    mlp_branch = matmul(active, down_weight) + down_bias
    return hidden + low_back(attn_branch + mlp_branch)

def reference(tokens, norm_gain_one, norm_shift_one, norm_gain_two, norm_shift_two, attn_in_weight, attn_in_bias, attn_out_weight, attn_out_bias, mlp_in_weight, mlp_in_bias, mlp_out_weight, mlp_out_bias, cotangent):
    params = (norm_gain_one.astype(jnp.float32), norm_shift_one.astype(jnp.float32), norm_gain_two.astype(jnp.float32), norm_shift_two.astype(jnp.float32), attn_in_weight.astype(jnp.float32), attn_in_bias.astype(jnp.float32), attn_out_weight.astype(jnp.float32), attn_out_bias.astype(jnp.float32), mlp_in_weight.astype(jnp.float32), mlp_in_bias.astype(jnp.float32), mlp_out_weight.astype(jnp.float32), mlp_out_bias.astype(jnp.float32))

    def forward(hidden, weights):
        for layer_index in range(LAYERS):
            hidden = layer(hidden, tuple((member[layer_index] for member in weights)))
        return hidden
    inputs = tokens.astype(jnp.float32).reshape(SEQUENCES // SEQS, SEQS, LEN, D)
    cotans = cotangent.astype(jnp.float32).reshape(SEQUENCES // SEQS, SEQS, LEN, D)

    def scan_step(totals, pair):
        batch_seqs, cotan_seqs = pair
        result, pullback = jax.vjp(forward, batch_seqs, params)
        hidden_grad, weight_grads = pullback(cotan_seqs)
        totals = jax.tree.map(lambda total, extra: total + extra, totals, weight_grads)
        return (totals, (result, hidden_grad))
    zero_totals = tuple((jnp.zeros_like(member) for member in params))
    totals, (results, hidden_grads) = lax.scan(scan_step, zero_totals, (inputs, cotans))
    output = results.reshape(SEQUENCES, LEN, D).astype(jnp.bfloat16)
    input_grad = hidden_grads.reshape(SEQUENCES, LEN, D).astype(jnp.bfloat16)
    return (output, input_grad, totals[0], totals[1], totals[2], totals[3], totals[4], totals[5], totals[6], totals[7], totals[8], totals[9], totals[10], totals[11])
```

```python
from functools import partial

import jax
import jax.numpy as jnp
from jax import lax
from jax.experimental import pallas as pl
from jax.experimental.pallas import tpu as pltpu
from jax.sharding import PartitionSpec as P

HEADS = 12
HEAD_DIM = 64
ROT = 16
LANES = 128
BF = jnp.bfloat16
F32 = jnp.float32

epsilon = 1e-05
VMEM_ASK = 48 * 1024 * 1024


def layer_norm(values, gain, shift):
    centre = jnp.mean(values, axis=-1, keepdims=True)
    centred = values - centre
    spread = jnp.mean(centred * centred, axis=-1, keepdims=True)
    return centred * lax.rsqrt(spread + epsilon) * gain + shift


def rotary_tables(positions):
    half_rot = ROT // 2
    inverse = 1.0 / 10000.0 ** (jnp.arange(half_rot, dtype=F32) * 2.0 / ROT)
    angles = positions.astype(F32)[:, None] * inverse[None, :]
    cosine, sine = jnp.cos(angles), jnp.sin(angles)
    rest = HEAD_DIM - ROT
    count = positions.shape[0]
    ones, zeros = jnp.ones((count, rest), F32), jnp.zeros((count, rest), F32)
    blank = jnp.zeros_like(sine)
    keep = jnp.concatenate([cosine, cosine, ones] * 2, axis=1)
    upper = jnp.concatenate([-sine, blank, zeros] * 2, axis=1)
    lower = jnp.concatenate([blank, sine, zeros] * 2, axis=1)
    return keep, upper, lower


def turn(values, keep, upper, lower):
    half_rot = ROT // 2
    return (
        values * keep
        + pltpu.roll(values, LANES - half_rot, axis=1) * upper
        + pltpu.roll(values, half_rot, axis=1) * lower
    )


def project_kernel(rotated_blocks, x_ref, w_ref, b_ref, keep_ref, upper_ref, lower_ref, o_ref):
    result = jnp.dot(x_ref[...], w_ref[...], preferred_element_type=F32) + b_ref[...]
    width = o_ref.shape[-1]

    @pl.when(pl.program_id(0) < rotated_blocks)
    def _():
        for start in range(0, width, LANES):
            part = turn(result[:, start : start + LANES], keep_ref[...], upper_ref[...], lower_ref[...])
            o_ref[0, :, start : start + LANES] = part.astype(BF)

    @pl.when(pl.program_id(0) >= rotated_blocks)
    def _():
        o_ref[0] = result.astype(BF)


def project(normed, weight, bias, tables, parts):
    rows, depth = normed.shape
    width = depth // parts
    blocks = 3 * parts
    table_spec = pl.BlockSpec((rows, LANES), lambda j: (0, 0))
    return pl.pallas_call(
        partial(project_kernel, 2 * parts),
        grid=(blocks,),
        in_specs=[
            pl.BlockSpec((rows, depth), lambda j: (0, 0)),
            pl.BlockSpec((depth, width), lambda j: (0, j)),
            pl.BlockSpec((1, width), lambda j: (0, j)),
            table_spec,
            table_spec,
            table_spec,
        ],
        out_specs=pl.BlockSpec((1, rows, width), lambda j: (j, 0, 0)),
        out_shape=jax.ShapeDtypeStruct((blocks, rows, width), BF),
        compiler_params=pltpu.CompilerParams(vmem_limit_bytes=VMEM_ASK),
        cost_estimate=pl.CostEstimate(
            flops=2 * rows * depth * 3 * depth, bytes_accessed=2 * (3 * depth * depth + 4 * rows * depth), transcendentals=0
        ),
    )(normed, weight, bias.astype(F32)[None, :], *tables)


NT = (((1,), (1,)), ((), ()))
TN = (((0,), (0,)), ((), ()))
SCALE = HEAD_DIM ** (-0.5)


def attend_kernel(block, q_ref, k_ref, v_ref, o_ref):
    length = q_ref.shape[1]
    visible = lax.broadcasted_iota(jnp.int32, (block, block), 0) >= lax.broadcasted_iota(
        jnp.int32, (block, block), 1
    )
    for head in range(LANES // HEAD_DIM):
        lanes = slice(head * HEAD_DIM, (head + 1) * HEAD_DIM)
        for start in range(0, length, block):
            end = start + block
            query = q_ref[0, start:end, lanes] * jnp.asarray(SCALE, BF)
            scores = lax.dot_general(query, k_ref[0, :end, lanes], NT, preferred_element_type=F32)
            last = jnp.where(visible, scores[:, start:], -jnp.inf)
            scores = last if start == 0 else jnp.concatenate([scores[:, :start], last], axis=1)
            raised = jnp.exp(scores - jnp.max(scores, axis=1, keepdims=True))
            chances = raised * (1.0 / jnp.sum(raised, axis=1, keepdims=True))
            mixed = jnp.dot(chances.astype(BF), v_ref[0, :end, lanes], preferred_element_type=F32)
            o_ref[start:end, lanes] = mixed.astype(BF)


def attend(qkv):
    _, length, width = qkv.shape
    block = min(256, length)
    specs = [pl.BlockSpec((1, length, LANES), lambda p, part=part: (part, 0, p)) for part in range(3)]
    return pl.pallas_call(
        partial(attend_kernel, block),
        grid=(width // LANES,),
        in_specs=specs,
        out_specs=pl.BlockSpec((length, LANES), lambda p: (0, p)),
        out_shape=jax.ShapeDtypeStruct((length, width), BF),
        compiler_params=pltpu.CompilerParams(vmem_limit_bytes=VMEM_ASK),
        cost_estimate=pl.CostEstimate(
            flops=4 * 4 * length * length * width, bytes_accessed=8 * length * width, transcendentals=length * length * width // HEAD_DIM
        ),
    )(qkv, qkv, qkv)


def attend_back_kernel(block, q_ref, k_ref, v_ref, g_ref, keep_ref, upper_ref, lower_ref, o_ref, dq, dk, dv):
    length = q_ref.shape[1]
    visible = lax.broadcasted_iota(jnp.int32, (block, block), 0) <= lax.broadcasted_iota(
        jnp.int32, (block, block), 1
    )
    for head in range(LANES // HEAD_DIM):
        lanes = slice(head * HEAD_DIM, (head + 1) * HEAD_DIM)
        for start in reversed(range(0, length, block)):
            end = start + block
            query = q_ref[0, start:end, lanes] * jnp.asarray(SCALE, BF)
            grad = g_ref[start:end, lanes]
            keys = k_ref[0, :end, lanes]
            scores = lax.dot_general(keys, query, NT, preferred_element_type=F32)
            last = jnp.where(visible, scores[start:], -jnp.inf)
            scores = last if start == 0 else jnp.concatenate([scores[:start], last], axis=0)
            raised = jnp.exp(scores - jnp.max(scores, axis=0, keepdims=True))
            chances = raised * (1.0 / jnp.sum(raised, axis=0, keepdims=True))
            grad_chances = lax.dot_general(v_ref[0, :end, lanes], grad, NT, preferred_element_type=F32)
            inner = jnp.sum(chances * grad_chances, axis=0, keepdims=True)
            grad_scores = (chances * (grad_chances - inner)).astype(BF)
            add_v = jnp.dot(chances.astype(BF), grad, preferred_element_type=F32)
            add_k = jnp.dot(grad_scores, query, preferred_element_type=F32)
            if end == length:
                dv[:, lanes] = add_v
                dk[:, lanes] = add_k
            else:
                dv[:end, lanes] += add_v
                dk[:end, lanes] += add_k
            dq[start:end, lanes] = lax.dot_general(grad_scores, keys, TN, preferred_element_type=F32) * SCALE
    keep, upper, lower = keep_ref[...], -upper_ref[...], -lower_ref[...]
    o_ref[0] = turn(dq[...], keep, upper, lower).astype(BF)
    o_ref[1] = turn(dk[...], keep, upper, lower).astype(BF)
    o_ref[2] = dv[...].astype(BF)


def attend_back(qkv, grad_context, tables):
    _, length, width = qkv.shape
    block = min(256, length)
    specs = [pl.BlockSpec((1, length, LANES), lambda p, part=part: (part, 0, p)) for part in range(3)]
    table_spec = pl.BlockSpec((length, LANES), lambda p: (0, 0))
    return pl.pallas_call(
        partial(attend_back_kernel, block),
        grid=(width // LANES,),
        in_specs=specs + [pl.BlockSpec((length, LANES), lambda p: (0, p))] + [table_spec] * 3,
        out_specs=pl.BlockSpec((3, length, LANES), lambda p: (0, 0, p)),
        out_shape=jax.ShapeDtypeStruct((3, length, width), BF),
        scratch_shapes=[pltpu.VMEM((length, LANES), F32)] * 3,
        compiler_params=pltpu.CompilerParams(vmem_limit_bytes=VMEM_ASK),
        cost_estimate=pl.CostEstimate(
            flops=4 * 10 * length * length * width, bytes_accessed=14 * length * width, transcendentals=length * length * width // HEAD_DIM
        ),
    )(qkv, qkv, qkv, grad_context, *tables)


def shards(
    tokens,
    norm_gain_one,
    norm_shift_one,
    norm_gain_two,
    norm_shift_two,
    attn_in_weight,
    attn_in_bias,
    attn_out_weight,
    attn_out_bias,
    mlp_in_weight,
    mlp_in_bias,
    mlp_out_weight,
    mlp_out_bias,
    cotangent,
):
    seq_count, stretch, width = tokens.shape
    rows = seq_count * stretch
    layers = norm_gain_one.shape[0]
    ctx_size = lax.axis_size("ctx")
    shard_size = lax.axis_size("shard")
    owners = shard_size * ctx_size
    length = stretch * ctx_size
    half = width // ctx_size
    at = lax.axis_index("ctx")
    shard_at = lax.axis_index("shard")
    both = ("shard", "ctx")
    tables = rotary_tables(jnp.arange(length, dtype=jnp.int32))
    own_tables = tuple(lax.dynamic_slice_in_dim(t, at * stretch, stretch, 0) for t in tables)
    swap = [(0, 1), (1, 0)]

    def ordered(mine, other, axis):
        return jnp.where(
            at == 0, jnp.concatenate([mine, other], axis=axis), jnp.concatenate([other, mine], axis=axis)
        )

    def trade(pieces, axis, join):
        mine = lax.dynamic_index_in_dim(pieces, at, axis, keepdims=False)
        theirs = lax.dynamic_index_in_dim(pieces, 1 - at, axis, keepdims=False)
        return ordered(mine, lax.ppermute(theirs, "ctx", swap), join)

    def halve(value, axis, bit, perm_axis, perm):
        mine = lax.dynamic_index_in_dim(value, bit, axis, keepdims=False)
        theirs = lax.dynamic_index_in_dim(value, 1 - bit, axis, keepdims=False)
        came = lax.ppermute(theirs, perm_axis, perm)
        return (mine.astype(F32) + came.astype(F32)).astype(BF)

    def flip(distance):
        return [(s, s ^ distance) for s in range(shard_size)]

    def scatter(value, x_first):
        tail = (value.shape[0] // owners,) + value.shape[1:]
        chips = shard_size // 2
        value = value.reshape((chips, 2, ctx_size) + tail)
        value = halve(value, 1, shard_at % 2, "shard", flip(1))
        if x_first:
            value = halve(value, 1, at, "ctx", swap)
        while chips > 1:
            chips //= 2
            value = value.reshape((2, chips) + value.shape[1:])
            value = halve(value, 0, (shard_at // 2 // chips) % 2, "shard", flip(2 * chips))
        value = value[0]
        if not x_first:
            value = halve(value, 0, at, "ctx", swap)
        return value

    small_list = (
        norm_gain_one,
        norm_shift_one,
        norm_gain_two,
        norm_shift_two,
        attn_in_bias,
        attn_out_bias,
        mlp_in_bias,
        mlp_out_bias,
    )
    small_own = jnp.concatenate([s.reshape(-1) for s in small_list])
    small_rows = -(-small_own.shape[0] // (8 * width)) * 8
    small_own = jnp.pad(small_own, (0, small_rows * width - small_own.shape[0])).reshape(small_rows, width)
    out_rows = attn_out_weight.shape[1]

    def gather(value):
        return lax.all_gather(value, both, axis=0, tiled=True)

    first = gather(jnp.concatenate([small_own, attn_out_weight[0]], axis=0))
    first = first.reshape(owners, small_rows + out_rows, width)
    small_all = first[:, :small_rows].reshape(owners, small_rows * width)
    smalls, offset = [], 0
    for s in small_list:
        count = s.shape[0] * s.shape[1]
        part = small_all[:, offset : offset + count].reshape(owners, layers, s.shape[1])
        smalls.append(part.transpose(1, 0, 2).reshape(layers, owners * s.shape[1]).astype(F32))
        offset += count
    gain_one, shift_one, gain_two, shift_two, in_bias, out_bias, up_bias, down_bias = smalls

    hidden = tokens.reshape(rows, width).astype(F32)
    stored = []
    for layer in range(layers):
        in_weight = gather(attn_in_weight[layer])
        up_weight = gather(mlp_in_weight[layer])
        down_weight = gather(mlp_out_weight[layer])
        if layer == 0:
            out_weight = first[:, small_rows:].reshape(width, width)
        else:
            out_weight = gather(attn_out_weight[layer])
        normed_one = layer_norm(hidden, gain_one[layer], shift_one[layer]).astype(BF)
        normed_two = layer_norm(hidden, gain_two[layer], shift_two[layer]).astype(BF)
        qkv_parts = project(normed_one, in_weight, in_bias[layer], own_tables, ctx_size)
        qkv = trade(qkv_parts.reshape(3, ctx_size, rows, half), 1, 1)
        pre_active = jnp.dot(normed_two, up_weight, preferred_element_type=F32) + up_bias[layer]
        active = jax.nn.gelu(pre_active, approximate=False).astype(BF)
        mixed = attend(qkv)
        context = trade(mixed.reshape(ctx_size, stretch, half), 0, 1)
        mlp_branch = jnp.dot(active, down_weight, preferred_element_type=F32) + down_bias[layer]
        attn_branch = jnp.dot(context, out_weight, preferred_element_type=F32) + out_bias[layer]
        stored.append(
            (hidden, normed_one, normed_two, qkv, context, pre_active, active, in_weight, out_weight, up_weight, down_weight)
        )
        hidden = hidden + (attn_branch + mlp_branch)
    output = hidden.astype(BF).reshape(seq_count, stretch, width)

    gradient = cotangent.reshape(rows, width).astype(F32)
    collected = [None] * layers
    previous = None
    for layer in reversed(range(layers)):
        (kept, normed_one, normed_two, qkv, context, pre_active, active, in_weight, out_weight, up_weight, down_weight) = (
            stored[layer]
        )
        grad_low = gradient.astype(BF)
        grad_context = jnp.einsum("re,de->rd", grad_low, out_weight, preferred_element_type=F32).astype(BF)
        grad_mixed = trade(grad_context.reshape(rows, ctx_size, half), 1, 0)
        grad_active = jnp.einsum("re,fe->rf", grad_low, down_weight, preferred_element_type=F32)
        unused, gelu_pull = jax.vjp(partial(jax.nn.gelu, approximate=False), pre_active)
        grad_pre = gelu_pull(grad_active)[0].astype(BF)
        grad_up = jnp.einsum("rd,rf->df", normed_two, grad_pre, preferred_element_type=F32).astype(BF)
        grad_down = jnp.einsum("rf,re->fe", active, grad_low, preferred_element_type=F32).astype(BF)
        grad_out = jnp.einsum("rd,re->de", context, grad_low, preferred_element_type=F32).astype(BF)
        up_share = scatter(grad_up, True)
        down_share = scatter(grad_down, False)
        out_share = scatter(grad_out, False)
        grad_normed_two = jnp.einsum("rf,df->rd", grad_pre, up_weight, preferred_element_type=F32)
        grad_qkv = attend_back(qkv, grad_mixed, tables)
        grad_sent = trade(grad_qkv.reshape(3, ctx_size, stretch, half), 1, 2)
        grad_projected = jnp.concatenate([grad_sent[0], grad_sent[1], grad_sent[2]], axis=1)
        grad_in = jnp.einsum("rd,re->de", normed_one, grad_projected, preferred_element_type=F32).astype(BF)
        in_cut = grad_in.shape[1] // 2
        in_share = jnp.concatenate([scatter(grad_in[:, :in_cut], True), scatter(grad_in[:, in_cut:], False)], axis=1)
        grad_normed_one = jnp.einsum("re,de->rd", grad_projected, in_weight, preferred_element_type=F32)
        unused, norm_pull_one = jax.vjp(layer_norm, kept, gain_one[layer], shift_one[layer])
        grad_hidden_one, grad_gain_one, grad_shift_one = norm_pull_one(grad_normed_one)
        unused, norm_pull_two = jax.vjp(layer_norm, kept, gain_two[layer], shift_two[layer])
        grad_hidden_two, grad_gain_two, grad_shift_two = norm_pull_two(grad_normed_two)
        small_grads = (
            grad_gain_one,
            grad_shift_one,
            grad_gain_two,
            grad_shift_two,
            jnp.sum(grad_projected.astype(F32), axis=0),
            jnp.sum(grad_low.astype(F32), axis=0),
            jnp.sum(grad_pre.astype(F32), axis=0),
        )
        gradient = gradient + grad_hidden_one + grad_hidden_two
        small = jnp.concatenate([s.astype(BF).reshape(owners, -1) for s in small_grads], axis=1)
        small_count = small.shape[1]
        small_share = scatter(small, True)
        last_width = in_share.shape[1]
        extra = -(-small_count // (8 * last_width)) * 8
        small_share = jnp.pad(small_share.reshape(-1), (0, extra * last_width - small_count))
        in_share = jnp.concatenate([in_share, small_share.reshape(extra, last_width)], axis=0)
        pack = (in_share, out_share, up_share, down_share)
        if previous is not None:
            pack, previous = lax.optimization_barrier((pack, previous))
            collected[layer + 1] = previous
        previous = lax.psum(pack, "replica")
        collected[layer] = (previous, tuple(s.shape[0] // owners for s in small_grads))
        if layer + 1 < layers:
            collected[layer + 1] = (collected[layer + 1], collected[layer][1])
    input_grad = gradient.astype(BF).reshape(seq_count, stretch, width)

    results = [[] for _ in range(12)]
    for layer in range(layers):
        (in_share, out_share, up_share, down_share), counts = collected[layer]
        in_rows = attn_in_weight.shape[1]
        flat = in_share[in_rows:].reshape(-1)
        parts, offset = [], 0
        for count in counts:
            parts.append(flat[offset : offset + count])
            offset += count
        g1, s1, g2, s2, b_in, b_branch, b_up = parts
        for slot, value in enumerate(
            (g1, s1, g2, s2, in_share[:in_rows], b_in, out_share, b_branch, up_share, b_up, down_share, b_branch)
        ):
            results[slot].append(value.astype(F32))
    return (output, input_grad) + tuple(jnp.stack(values) for values in results)


def solution(mesh):
    rows_spec = P(("replica", "shard"), "ctx", None)
    vector = P(None, ("shard", "ctx"))
    matrix = P(None, ("shard", "ctx"), None)
    params = (vector,) * 4 + (matrix, vector) * 4
    return jax.shard_map(
        shards,
        mesh=mesh,
        in_specs=(rows_spec,) + params + (rows_spec,),
        out_specs=(rows_spec, rows_spec) + params,
        check_vma=False,
    )
```

```python
import math
from functools import partial

import jax
import jax.numpy as jnp
from jax import lax
from jax.experimental import pallas as pl
from jax.experimental.pallas import tpu as pltpu
from jax.sharding import PartitionSpec as P

HEADS = 12
HEAD_DIM = 64
ROT = 16
LANES = 128
BF = jnp.bfloat16
F32 = jnp.float32

epsilon = 1e-05
VMEM_ASK = 48 * 1024 * 1024


def layer_norm(values, gain, shift):
    centre = jnp.mean(values, axis=-1, keepdims=True)
    centred = values - centre
    spread = jnp.mean(centred * centred, axis=-1, keepdims=True)
    return centred * lax.rsqrt(spread + epsilon) * gain + shift


def below(values):
    return (lax.erf(values * 0.5**0.5) + 1.0) * 0.5


def rotary_tables(positions):
    half_rot = ROT // 2
    inverse = 1.0 / 10000.0 ** (jnp.arange(half_rot, dtype=F32) * 2.0 / ROT)
    angles = positions.astype(F32)[:, None] * inverse[None, :]
    cosine, sine = jnp.cos(angles), jnp.sin(angles)
    rest = HEAD_DIM - ROT
    count = positions.shape[0]
    ones, zeros = jnp.ones((count, rest), F32), jnp.zeros((count, rest), F32)
    blank = jnp.zeros_like(sine)
    keep = jnp.concatenate([cosine, cosine, ones] * 2, axis=1)
    upper = jnp.concatenate([-sine, blank, zeros] * 2, axis=1)
    lower = jnp.concatenate([blank, sine, zeros] * 2, axis=1)
    return keep, upper, lower


def turn(values, keep, upper, lower):
    half_rot = ROT // 2
    return (
        values * keep
        + pltpu.roll(values, LANES - half_rot, axis=1) * upper
        + pltpu.roll(values, half_rot, axis=1) * lower
    )


def project_kernel(rotated_blocks, x_ref, w_ref, b_ref, keep_ref, upper_ref, lower_ref, o_ref):
    result = jnp.dot(x_ref[...], w_ref[...], preferred_element_type=F32) + b_ref[...]
    width = o_ref.shape[-1]

    @pl.when(pl.program_id(0) < rotated_blocks)
    def _():
        for start in range(0, width, LANES):
            part = turn(result[:, start : start + LANES], keep_ref[...], upper_ref[...], lower_ref[...])
            o_ref[0, :, start : start + LANES] = part.astype(BF)

    @pl.when(pl.program_id(0) >= rotated_blocks)
    def _():
        o_ref[0] = result.astype(BF)


def project(normed, weight, bias, tables, parts):
    rows, depth = normed.shape
    width = depth // parts
    blocks = 3 * parts
    table_spec = pl.BlockSpec((rows, LANES), lambda j: (0, 0))
    return pl.pallas_call(
        partial(project_kernel, 2 * parts),
        grid=(blocks,),
        in_specs=[
            pl.BlockSpec((rows, depth), lambda j: (0, 0)),
            pl.BlockSpec((depth, width), lambda j: (0, j)),
            pl.BlockSpec((1, width), lambda j: (0, j)),
            table_spec,
            table_spec,
            table_spec,
        ],
        out_specs=pl.BlockSpec((1, rows, width), lambda j: (j, 0, 0)),
        out_shape=jax.ShapeDtypeStruct((blocks, rows, width), BF),
        compiler_params=pltpu.CompilerParams(vmem_limit_bytes=VMEM_ASK),
        cost_estimate=pl.CostEstimate(
            flops=2 * rows * depth * 3 * depth, bytes_accessed=2 * (3 * depth * depth + 4 * rows * depth), transcendentals=0
        ),
    )(normed, weight, bias.astype(F32)[None, :], *tables)


NT = (((1,), (1,)), ((), ()))
TN = (((0,), (0,)), ((), ()))
SCALE = HEAD_DIM ** (-0.5)


def attend_kernel(block, q_ref, k_ref, v_ref, o_ref):
    length = q_ref.shape[1]
    visible = lax.broadcasted_iota(jnp.int32, (block, block), 0) >= lax.broadcasted_iota(
        jnp.int32, (block, block), 1
    )
    for head in range(LANES // HEAD_DIM):
        lanes = slice(head * HEAD_DIM, (head + 1) * HEAD_DIM)
        for start in range(0, length, block):
            end = start + block
            query = q_ref[0, start:end, lanes] * jnp.asarray(SCALE, BF)
            scores = lax.dot_general(query, k_ref[0, :end, lanes], NT, preferred_element_type=F32)
            last = jnp.where(visible, scores[:, start:], -jnp.inf)
            scores = last if start == 0 else jnp.concatenate([scores[:, :start], last], axis=1)
            raised = jnp.exp(scores - jnp.max(scores, axis=1, keepdims=True))
            chances = raised * (1.0 / jnp.sum(raised, axis=1, keepdims=True))
            mixed = jnp.dot(chances.astype(BF), v_ref[0, :end, lanes], preferred_element_type=F32)
            o_ref[start:end, lanes] = mixed.astype(BF)


def attend(qkv):
    _, length, width = qkv.shape
    block = min(256, length)
    specs = [pl.BlockSpec((1, length, LANES), lambda p, part=part: (part, 0, p)) for part in range(3)]
    return pl.pallas_call(
        partial(attend_kernel, block),
        grid=(width // LANES,),
        in_specs=specs,
        out_specs=pl.BlockSpec((length, LANES), lambda p: (0, p)),
        out_shape=jax.ShapeDtypeStruct((length, width), BF),
        compiler_params=pltpu.CompilerParams(vmem_limit_bytes=VMEM_ASK),
        cost_estimate=pl.CostEstimate(
            flops=4 * 4 * length * length * width, bytes_accessed=8 * length * width, transcendentals=length * length * width // HEAD_DIM
        ),
    )(qkv, qkv, qkv)


def attend_back_kernel(block, q_ref, k_ref, v_ref, g_ref, keep_ref, upper_ref, lower_ref, o_ref, dq, dk, dv):
    length = q_ref.shape[1]
    visible = lax.broadcasted_iota(jnp.int32, (block, block), 0) <= lax.broadcasted_iota(
        jnp.int32, (block, block), 1
    )
    for head in range(LANES // HEAD_DIM):
        lanes = slice(head * HEAD_DIM, (head + 1) * HEAD_DIM)
        for start in reversed(range(0, length, block)):
            end = start + block
            query = q_ref[0, start:end, lanes] * jnp.asarray(SCALE, BF)
            grad = g_ref[start:end, lanes]
            keys = k_ref[0, :end, lanes]
            scores = lax.dot_general(keys, query, NT, preferred_element_type=F32)
            last = jnp.where(visible, scores[start:], -jnp.inf)
            scores = last if start == 0 else jnp.concatenate([scores[:start], last], axis=0)
            raised = jnp.exp(scores - jnp.max(scores, axis=0, keepdims=True))
            chances = raised * (1.0 / jnp.sum(raised, axis=0, keepdims=True))
            grad_chances = lax.dot_general(v_ref[0, :end, lanes], grad, NT, preferred_element_type=F32)
            inner = jnp.sum(chances * grad_chances, axis=0, keepdims=True)
            grad_scores = (chances * (grad_chances - inner)).astype(BF)
            add_v = jnp.dot(chances.astype(BF), grad, preferred_element_type=F32)
            add_k = jnp.dot(grad_scores, query, preferred_element_type=F32)
            if end == length:
                dv[:, lanes] = add_v
                dk[:, lanes] = add_k
            else:
                dv[:end, lanes] += add_v
                dk[:end, lanes] += add_k
            dq[start:end, lanes] = lax.dot_general(grad_scores, keys, TN, preferred_element_type=F32) * SCALE
    keep, upper, lower = keep_ref[...], -upper_ref[...], -lower_ref[...]
    o_ref[0] = turn(dq[...], keep, upper, lower).astype(BF)
    o_ref[1] = turn(dk[...], keep, upper, lower).astype(BF)
    o_ref[2] = dv[...].astype(BF)


def attend_back(qkv, grad_context, tables):
    _, length, width = qkv.shape
    block = min(256, length)
    specs = [pl.BlockSpec((1, length, LANES), lambda p, part=part: (part, 0, p)) for part in range(3)]
    table_spec = pl.BlockSpec((length, LANES), lambda p: (0, 0))
    return pl.pallas_call(
        partial(attend_back_kernel, block),
        grid=(width // LANES,),
        in_specs=specs + [pl.BlockSpec((length, LANES), lambda p: (0, p))] + [table_spec] * 3,
        out_specs=pl.BlockSpec((3, length, LANES), lambda p: (0, 0, p)),
        out_shape=jax.ShapeDtypeStruct((3, length, width), BF),
        scratch_shapes=[pltpu.VMEM((length, LANES), F32)] * 3,
        compiler_params=pltpu.CompilerParams(vmem_limit_bytes=VMEM_ASK),
        cost_estimate=pl.CostEstimate(
            flops=4 * 10 * length * length * width, bytes_accessed=14 * length * width, transcendentals=length * length * width // HEAD_DIM
        ),
    )(qkv, qkv, qkv, grad_context, *tables)


def shards(
    tokens,
    norm_gain_one,
    norm_shift_one,
    norm_gain_two,
    norm_shift_two,
    attn_in_weight,
    attn_in_bias,
    attn_out_weight,
    attn_out_bias,
    mlp_in_weight,
    mlp_in_bias,
    mlp_out_weight,
    mlp_out_bias,
    cotangent,
):
    seq_count, stretch, width = tokens.shape
    rows = seq_count * stretch
    layers = norm_gain_one.shape[0]
    ctx_size = lax.axis_size("ctx")
    shard_size = lax.axis_size("shard")
    owners = shard_size * ctx_size
    length = stretch * ctx_size
    half = width // ctx_size
    at = lax.axis_index("ctx")
    shard_at = lax.axis_index("shard")
    both = ("shard", "ctx")
    tables = rotary_tables(jnp.arange(length, dtype=jnp.int32))
    own_tables = tuple(lax.dynamic_slice_in_dim(t, at * stretch, stretch, 0) for t in tables)
    swap = [(0, 1), (1, 0)]

    def ordered(mine, other, axis):
        return jnp.where(
            at == 0, jnp.concatenate([mine, other], axis=axis), jnp.concatenate([other, mine], axis=axis)
        )

    def trade(pieces, axis, join):
        mine = lax.dynamic_index_in_dim(pieces, at, axis, keepdims=False)
        theirs = lax.dynamic_index_in_dim(pieces, 1 - at, axis, keepdims=False)
        return ordered(mine, lax.ppermute(theirs, "ctx", swap), join)

    def halve(value, axis, bit, perm_axis, perm):
        mine = lax.dynamic_index_in_dim(value, bit, axis, keepdims=False)
        theirs = lax.dynamic_index_in_dim(value, 1 - bit, axis, keepdims=False)
        came = lax.ppermute(theirs, perm_axis, perm)
        return (mine.astype(F32) + came.astype(F32)).astype(BF)

    def flip(distance):
        return [(s, s ^ distance) for s in range(shard_size)]

    def scatter_steps(value, x_first):
        tail = (value.shape[0] // owners,) + value.shape[1:]
        chips = shard_size // 2
        value = value.reshape((chips, 2, ctx_size) + tail)
        value = halve(value, 1, shard_at % 2, "shard", flip(1))
        value = yield value
        if x_first:
            value = halve(value, 1, at, "ctx", swap)
            value = yield value
        while chips > 1:
            chips //= 2
            value = value.reshape((2, chips) + value.shape[1:])
            value = halve(value, 0, (shard_at // 2 // chips) % 2, "shard", flip(2 * chips))
            value = yield value
        if not x_first:
            value = halve(value, 1, at, "ctx", swap)
            value = yield value
        yield value[0]

    def drain(steps, value):
        while True:
            try:
                value = steps.send(value)
            except StopIteration:
                return value

    def scatter(value, x_first):
        steps = scatter_steps(value, x_first)
        return drain(steps, next(steps))

    small_list = (
        norm_gain_one,
        norm_shift_one,
        norm_gain_two,
        norm_shift_two,
        attn_in_bias,
        attn_out_bias,
        mlp_in_bias,
        mlp_out_bias,
    )
    small_own = jnp.concatenate([s.reshape(-1) for s in small_list])
    in_width = attn_in_weight.shape[2]
    wide = in_width + width
    small_rows = -(-small_own.shape[0] // (8 * wide)) * 8
    small_own = jnp.pad(small_own, (0, small_rows * wide - small_own.shape[0])).reshape(small_rows, wide)
    out_rows = attn_out_weight.shape[1]

    def gather(value):
        return lax.all_gather(value, both, axis=0, tiled=True)

    def side_by_side(layer):
        return jnp.concatenate([attn_in_weight[layer], attn_out_weight[layer]], axis=1)

    first = gather(jnp.concatenate([small_own, side_by_side(0)], axis=0))
    first = first.reshape(owners, small_rows + out_rows, wide)
    small_all = first[:, :small_rows].reshape(owners, small_rows * wide)
    smalls, offset = [], 0
    for s in small_list:
        count = s.shape[0] * s.shape[1]
        part = small_all[:, offset : offset + count].reshape(owners, layers, s.shape[1])
        smalls.append(part.transpose(1, 0, 2).reshape(layers, owners * s.shape[1]).astype(F32))
        offset += count
    gain_one, shift_one, gain_two, shift_two, in_bias, out_bias, up_bias, down_bias = smalls

    hidden = tokens.reshape(rows, width).astype(F32)
    stored = []
    for layer in range(layers):
        if layer == 0:
            attn_weights = first[:, small_rows:].reshape(width, wide)
        else:
            attn_weights = gather(side_by_side(layer))
        up_weight = gather(mlp_in_weight[layer])
        down_weight = gather(mlp_out_weight[layer])
        in_weight, out_weight = attn_weights[:, :in_width], attn_weights[:, in_width:]
        normed_one = layer_norm(hidden, gain_one[layer], shift_one[layer]).astype(BF)
        normed_two = layer_norm(hidden, gain_two[layer], shift_two[layer]).astype(BF)
        qkv_parts = project(normed_one, attn_weights, in_bias[layer], own_tables, ctx_size)
        qkv = trade(qkv_parts.reshape(3, ctx_size, rows, half), 1, 1)
        pre_active = jnp.dot(normed_two, up_weight, preferred_element_type=F32) + up_bias[layer]
        active = (pre_active * below(pre_active)).astype(BF)
        mixed = attend(qkv)
        context = trade(mixed.reshape(ctx_size, stretch, half), 0, 1)
        mlp_branch = jnp.dot(active, down_weight, preferred_element_type=F32) + down_bias[layer]
        attn_branch = jnp.dot(context, out_weight, preferred_element_type=F32) + out_bias[layer]
        stored.append(
            (hidden, normed_one, normed_two, qkv, context, pre_active, active, in_weight, out_weight, up_weight, down_weight)
        )
        hidden = hidden + (attn_branch + mlp_branch)
    output = hidden.astype(BF).reshape(seq_count, stretch, width)

    gradient = cotangent.reshape(rows, width).astype(F32)
    collected = [None] * layers
    previous, waiting = None, ()
    for layer in reversed(range(layers)):
        (kept, normed_one, normed_two, qkv, context, pre_active, active, in_weight, out_weight, up_weight, down_weight) = (
            stored[layer]
        )
        grad_low = gradient.astype(BF)
        grad_context = jnp.einsum("re,de->rd", grad_low, out_weight, preferred_element_type=F32).astype(BF)
        grad_mixed = trade(grad_context.reshape(rows, ctx_size, half), 1, 0)
        grad_active = jnp.einsum("re,fe->rf", grad_low, down_weight, preferred_element_type=F32)
        density = jnp.exp(pre_active * pre_active * -0.5) * (2.0 * math.pi) ** -0.5
        grad_pre = (grad_active * (below(pre_active) + pre_active * density)).astype(BF)
        grad_up = jnp.einsum("rd,rf->df", normed_two, grad_pre, preferred_element_type=F32).astype(BF)
        grad_down = jnp.einsum("rf,re->fe", active, grad_low, preferred_element_type=F32).astype(BF)
        grad_out = jnp.einsum("rd,re->de", context, grad_low, preferred_element_type=F32).astype(BF)
        chains = [scatter_steps(grad_up, True), scatter_steps(grad_down, False), scatter_steps(grad_out, False)]
        held = [next(chain) for chain in chains]
        held, grad_mixed, waiting = lax.optimization_barrier((held, grad_mixed, waiting))
        if waiting:
            previous = lax.psum(waiting, "replica")
            collected[layer + 1] = (previous, collected[layer + 1][1])
        held = [chain.send(value) for chain, value in zip(chains, held)]
        grad_normed_two = jnp.einsum("rf,df->rd", grad_pre, up_weight, preferred_element_type=F32)
        grad_qkv = attend_back(qkv, grad_mixed, tables)
        grad_sent = trade(grad_qkv.reshape(3, ctx_size, stretch, half), 1, 2)
        held, grad_sent = lax.optimization_barrier((held, grad_sent))
        up_share, down_share, out_share = (drain(chain, value) for chain, value in zip(chains, held))
        grad_projected = jnp.concatenate([grad_sent[0], grad_sent[1], grad_sent[2]], axis=1)
        grad_in = jnp.einsum("rd,re->de", normed_one, grad_projected, preferred_element_type=F32).astype(BF)
        in_cut = grad_in.shape[1] // 2
        in_share = jnp.concatenate([scatter(grad_in[:, :in_cut], True), scatter(grad_in[:, in_cut:], False)], axis=1)
        grad_normed_one = jnp.einsum("re,de->rd", grad_projected, in_weight, preferred_element_type=F32)
        unused, norm_pull_one = jax.vjp(layer_norm, kept, gain_one[layer], shift_one[layer])
        grad_hidden_one, grad_gain_one, grad_shift_one = norm_pull_one(grad_normed_one)
        unused, norm_pull_two = jax.vjp(layer_norm, kept, gain_two[layer], shift_two[layer])
        grad_hidden_two, grad_gain_two, grad_shift_two = norm_pull_two(grad_normed_two)
        small_grads = (
            grad_gain_one,
            grad_shift_one,
            grad_gain_two,
            grad_shift_two,
            jnp.sum(grad_projected.astype(F32), axis=0),
            jnp.sum(grad_low.astype(F32), axis=0),
            jnp.sum(grad_pre.astype(F32), axis=0),
        )
        gradient = gradient + grad_hidden_one + grad_hidden_two
        small = jnp.concatenate([s.astype(BF).reshape(owners, -1) for s in small_grads], axis=1)
        small_count = small.shape[1]
        small_share = scatter(small, True)
        last_width = in_share.shape[1]
        extra = -(-small_count // (8 * last_width)) * 8
        small_share = jnp.pad(small_share.reshape(-1), (0, extra * last_width - small_count))
        in_share = jnp.concatenate([in_share, small_share.reshape(extra, last_width)], axis=0)
        sums = ()
        if layer > 0:
            waiting = (in_share, out_share, up_share, down_share)
        else:
            for group in ((out_share, up_share, down_share), (in_share,)):
                if previous is not None:
                    group, previous = lax.optimization_barrier((group, previous))
                previous = lax.psum(group, "replica")
                sums += previous
            sums = sums[-1:] + sums[:-1]
        collected[layer] = (sums, tuple(s.shape[0] // owners for s in small_grads))
    input_grad = gradient.astype(BF).reshape(seq_count, stretch, width)

    results = [[] for _ in range(12)]
    for layer in range(layers):
        (in_share, out_share, up_share, down_share), counts = collected[layer]
        in_rows = attn_in_weight.shape[1]
        flat = in_share[in_rows:].reshape(-1)
        parts, offset = [], 0
        for count in counts:
            parts.append(flat[offset : offset + count])
            offset += count
        g1, s1, g2, s2, b_in, b_branch, b_up = parts
        for slot, value in enumerate(
            (g1, s1, g2, s2, in_share[:in_rows], b_in, out_share, b_branch, up_share, b_up, down_share, b_branch)
        ):
            results[slot].append(value.astype(F32))
    return (output, input_grad) + tuple(jnp.stack(values) for values in results)


def solution(mesh):
    rows_spec = P(("replica", "shard"), "ctx", None)
    vector = P(None, ("shard", "ctx"))
    matrix = P(None, ("shard", "ctx"), None)
    params = (vector,) * 4 + (matrix, vector) * 4
    return jax.shard_map(
        shards,
        mesh=mesh,
        in_specs=(rows_spec,) + params + (rows_spec,),
        out_specs=(rows_spec, rows_spec) + params,
        check_vma=False,
    )
```
